512 devices in a mesh: node: 8 (over z), local: 64 (over x, y, core).
Axes of the slice: x: 4, y: 8, z: 8, core: 2. Of those that a mesh axis runs over, the one named last changes fastest.
Arguments:
- tokens: bfloat16 [4096, 7168], P('node', 'local'), may hold values from -6 to 6
- out_grad: bfloat16 [4096, 7168], P('node', 'local'), may hold values from -1.1953125 to 1.1953125
- route_ids: int32 [4096, 8], P('node'), may hold values from 0 to 255, as said below
- route_weights: float32 [4096, 8], P('node'), may hold values from 0.2 to 1
- gate_weight: bfloat16 [8, 64, 896, 256], P('node', 'local'), may hold values from -0.0625 to 0.0625
- up_weight: bfloat16 [8, 64, 896, 256], P('node', 'local'), may hold values from -0.0625 to 0.0625
- down_weight: bfloat16 [8, 64, 256, 896], P('node', 'local'), may hold values from -0.125 to 0.125
Outputs:
- layer_out: bfloat16 [4096, 7168], P('node', 'local')
- input_grad: bfloat16 [4096, 7168], P('node', 'local')
- gate_grad: bfloat16 [8, 64, 896, 256], P('node', 'local')
- up_grad: bfloat16 [8, 64, 896, 256], P('node', 'local')
- down_grad: bfloat16 [8, 64, 256, 896], P('node', 'local')
The draws below stay inside these ranges and needn't reach their ends.
Inputs may be any that keep to these rules, and one draw needn't show every extreme that they name: `route_ids`: each row names 8 different experts, all from 4 of the 8 blocks of 32 consecutive numbers. Call the multiples of 32 the computed experts. A row names at most one computed expert. Within each node group's 512 consecutive rows, each computed expert is named by at most 32 rows, and in every draw some computed expert is named by exactly 32 rows of every node group's rows.
All inputs are finite; a program needn't handle non-finite values.
Results may differ from the reference program's by a relative error of at most 0.0058.
Values may be sent and summed in bfloat16 or wider, within the bound.
A program may use at most 64 MiB of HBM per device.

```python
import jax
import jax.numpy as jnp
from jax import lax

D = 7168
HID = 2048
EXPERTS = 256
TOPK = 8
GROUPS = 8
TOPK_GROUP = 4
TOK_NODE = 512
CAP = 32
TOKENS = 4096
DA = 896
HB = 256
N_NODE = 8
N_LOCAL = 64


def draw_route_ids(key, part):
    key = jax.random.fold_in(key, 7)
    key_hot, key_shift, key_cut, key_place, key_group, key_pick = jax.random.split(key, 6)
    node_count = TOKENS // TOK_NODE
    stride = EXPERTS // node_count
    group_width = EXPERTS // GROUPS
    shifts = jax.random.randint(key_shift, (node_count,), 0, 4)
    hottest = jax.random.randint(key_hot, (), 0, node_count)
    is_hot = jnp.arange(node_count) == hottest
    shifts = jnp.where(is_hot, 0, shifts)
    base_counts = jnp.right_shift(jnp.full((node_count,), CAP, jnp.int32), shifts.astype(jnp.int32))
    cut_counts = jax.random.randint(key_cut, (node_count, node_count), 0, 1 << 20) % (base_counts[None, :] // 2 + 1)
    counts = base_counts[None, :] - jnp.where(is_hot[None, :], 0, cut_counts)
    place_keys = jax.random.split(key_place, node_count)
    places = jax.vmap(lambda one_key: jax.random.permutation(one_key, TOK_NODE))(place_keys).reshape(-1).astype(jnp.int32)
    owner_slot = places // CAP
    within = places % CAP
    node_of = jnp.arange(TOKENS, dtype=jnp.int32) // TOK_NODE
    safe_slot = jnp.minimum(owner_slot, node_count - 1)
    hit_row = (owner_slot < node_count) & (within < counts[node_of, safe_slot])
    resident = safe_slot * stride
    group_index = jnp.arange(GROUPS, dtype=jnp.int32)
    group_scores = jax.random.randint(key_group, (TOKENS, GROUPS), 0, 1 << 20) * GROUPS + group_index[None, :]
    group_scores = jnp.where(hit_row[:, None] & (group_index[None, :] == (resident // group_width)[:, None]), -1, group_scores)
    chosen = jnp.argsort(group_scores, axis=1)[:, :TOPK_GROUP]
    slot_index = jnp.arange(TOPK_GROUP * group_width, dtype=jnp.int32)
    spread_groups = jnp.broadcast_to((slot_index // group_width)[None, :], (TOKENS, TOPK_GROUP * group_width))
    candidates = jnp.take_along_axis(chosen, spread_groups, axis=1) * group_width + (slot_index % group_width)[None, :]
    pick_scores = jax.random.randint(key_pick, (TOKENS, TOPK_GROUP * group_width), 0, 1 << 20) * (TOPK_GROUP * group_width) + slot_index[None, :]
    pick_scores = jnp.where(candidates % stride == 0, 1 << 30, pick_scores)
    pick_scores = jnp.where(hit_row[:, None] & (candidates == resident[:, None]), -1, pick_scores)
    picked = jnp.argsort(pick_scores, axis=1)[:, :TOPK]
    return jnp.take_along_axis(candidates, picked, axis=1).astype(jnp.int32)


def block_levels(key, shape, cuts, least, largest):
    level, own = 1.0, jax.random.fold_in(key, 6)
    for dim, parts in cuts:
        steps = jnp.exp(jax.random.uniform(jax.random.fold_in(own, dim), (parts,), jnp.float32, least / len(cuts), largest / len(cuts)))
        level = level * jnp.repeat(steps, shape[dim] // parts).reshape([-1 if axis == dim else 1 for axis in range(len(shape))])
    return level


def bell_draw(key, extent, spread, bound, cuts=(), kind=jnp.bfloat16):
    level = block_levels(key, extent, cuts, -0.22, 0.18) if cuts else 1.0
    array = jax.random.normal(key, extent, jnp.float32) * spread * level
    return jnp.minimum(jnp.maximum(array, -bound), bound).astype(kind)


def setup_inputs(seed: int = 0) -> dict:
    streams_of = jax.random.split(jax.random.key(seed), 8)
    tokens = bell_draw(streams_of[0], (TOKENS, D), 1.0, 6.0, ((0, 8), (1, 64)))
    out_grad = bell_draw(streams_of[1], (TOKENS, D), 0.2, 1.1953125, ((0, 8), (1, 64)))
    route_ids = draw_route_ids(jax.random.fold_in(streams_of[7], 71), 0)
    route_weights = jnp.clip(0.2 + 0.8 * jax.random.uniform(streams_of[3], (TOKENS, TOPK), jnp.float32) ** block_levels(streams_of[3], (TOKENS, TOPK), ((0, 8),), -0.2, 0.2), 0.2, 1.0)
    gate_weight = bell_draw(streams_of[4], (N_NODE, N_LOCAL, DA, HB), D ** -0.5, 0.0625, ((0, 8), (1, 64)))
    up_weight = bell_draw(streams_of[5], (N_NODE, N_LOCAL, DA, HB), D ** -0.5, 0.0625, ((0, 8), (1, 64)))
    down_weight = bell_draw(streams_of[6], (N_NODE, N_LOCAL, HB, DA), HID ** -0.5, 0.125, ((0, 8), (1, 64)))
    return {"tokens": tokens, "out_grad": out_grad, "route_ids": route_ids, "route_weights": route_weights, "gate_weight": gate_weight, "up_weight": up_weight, "down_weight": down_weight}


def join_blocks(blocked):
    feature_parts = blocked.shape[0] // 8
    block_rows = blocked.shape[1]
    block_cols = blocked.shape[2]
    return blocked.reshape(feature_parts, 8, block_rows, block_cols).transpose(0, 2, 1, 3).reshape(feature_parts * block_rows, 8 * block_cols)


def join_down(blocked):
    feature_parts = blocked.shape[0] // 8
    block_rows = blocked.shape[1]
    block_cols = blocked.shape[2]
    return blocked.reshape(feature_parts, 8, block_rows, block_cols).transpose(1, 2, 0, 3).reshape(8 * block_rows, feature_parts * block_cols)


def split_blocks(matrix, feature_parts):
    block_rows = matrix.shape[0] // feature_parts
    block_cols = matrix.shape[1] // 8
    return matrix.reshape(feature_parts, block_rows, 8, block_cols).transpose(0, 2, 1, 3).reshape(feature_parts * 8, block_rows, block_cols)


def split_down(matrix, feature_parts):
    block_rows = matrix.shape[0] // 8
    block_cols = matrix.shape[1] // feature_parts
    return matrix.reshape(8, block_rows, feature_parts, block_cols).transpose(2, 0, 1, 3).reshape(feature_parts * 8, block_rows, block_cols)


def contract(left_side, right_side, left_dim, right_dim):
    return lax.dot_general(left_side, right_side, (((left_dim,), (right_dim,)), ((), ())), preferred_element_type=jnp.float32)


def reference(tokens, out_grad, route_ids, route_weights, gate_weight, up_weight, down_weight):
    groups = gate_weight.shape[0]
    feature_parts = gate_weight.shape[1] // 8
    row_count = CAP * groups
    owned_ids = jnp.arange(groups, dtype=jnp.int32) * (EXPERTS // groups)
    matches = route_ids[:, :, None] == owned_ids[None, None, :]
    hit_mask = jnp.any(matches, axis=1)
    shares = jnp.sum(jnp.where(matches, route_weights[:, :, None], jnp.zeros((), route_weights.dtype)), axis=1)
    layer_sum = jnp.zeros(tokens.shape, jnp.float32)
    input_sum = jnp.zeros(tokens.shape, jnp.float32)
    gate_list = []
    up_list = []
    down_list = []
    for owner_index in range(groups):
        row_index = jnp.nonzero(hit_mask[:, owner_index], size=row_count, fill_value=0)[0].astype(jnp.int32)
        live_rows = jnp.arange(row_count) < jnp.sum(hit_mask[:, owner_index].astype(jnp.int32))
        row_share = jnp.where(live_rows, shares[row_index, owner_index], jnp.zeros((), shares.dtype))
        expert_in = jnp.where(live_rows[:, None], tokens[row_index], jnp.zeros((), tokens.dtype))
        expert_grad = (row_share[:, None] * out_grad[row_index].astype(jnp.float32)).astype(jnp.bfloat16)
        w_gate = join_blocks(gate_weight[owner_index])
        w_up = join_blocks(up_weight[owner_index])
        w_down = join_down(down_weight[owner_index])
        gate_sum = jnp.dot(expert_in, w_gate, preferred_element_type=jnp.float32)
        up_sum = jnp.dot(expert_in, w_up, preferred_element_type=jnp.float32)
        sigmoid_gate = jax.nn.sigmoid(gate_sum)
        active = gate_sum * sigmoid_gate
        hidden = (active * up_sum).astype(jnp.bfloat16)
        expert_out = jnp.dot(hidden, w_down, preferred_element_type=jnp.float32).astype(jnp.bfloat16)
        back_sum = contract(expert_grad, w_down, 1, 1)
        grad_gate = (back_sum * up_sum * sigmoid_gate * (1.0 + gate_sum * (1.0 - sigmoid_gate))).astype(jnp.bfloat16)
        grad_up = (back_sum * active).astype(jnp.bfloat16)
        expert_back = (contract(grad_gate, w_gate, 1, 1) + contract(grad_up, w_up, 1, 1)).astype(jnp.bfloat16)
        layer_sum = layer_sum.at[row_index].add(row_share[:, None] * expert_out.astype(jnp.float32))
        input_sum = input_sum.at[row_index].add(jnp.where(live_rows[:, None], expert_back.astype(jnp.float32), jnp.zeros((), jnp.float32)))
        gate_list.append(split_blocks(contract(expert_in, grad_gate, 0, 0).astype(jnp.bfloat16), feature_parts))
        up_list.append(split_blocks(contract(expert_in, grad_up, 0, 0).astype(jnp.bfloat16), feature_parts))
        down_list.append(split_down(contract(hidden, expert_grad, 0, 0).astype(jnp.bfloat16), feature_parts))
    return (layer_sum.astype(jnp.bfloat16), input_sum.astype(jnp.bfloat16), jnp.stack(gate_list), jnp.stack(up_list), jnp.stack(down_list))
```

```python
import jax
import jax.numpy as jnp
from jax import lax
from jax.experimental import pallas as pl
from jax.experimental.pallas import tpu as pltpu
from jax.sharding import PartitionSpec as P

EXPERTS = 256
CAP = 32
NODES = 8
MESH = pl.DeviceIdType.MESH
BF16 = jnp.bfloat16
F32 = jnp.float32


def nn(left, right):
    return lax.dot_general(left, right, (((1,), (0,)), ((), ())), preferred_element_type=F32)


def nt(left, right):
    return lax.dot_general(left, right, (((1,), (1,)), ((), ())), preferred_element_type=F32)


def kernel(
    tok, og, ids, wts, wg_h, wu_h, wd_h,
    lo, ig, gg_h, ug_h, dg_h,
    wg, wu, wd, wgt, wut, wdt, sel, a_src, a_dst, pieces,
    c_own, c_src, c_dst, y_src, y_dst, rows, e_src, e_dst, r_own, r_src, r_dst, f_src, f_dst,
    gg, ug, dg,
    w_sem, o_sem, as_sem, ar_sem, bs_sem, br_sem, gs_sem, gr_sem, cs_sem, cr_sem, ys_sem, yr_sem,
    ds_sem, dr_sem, es_sem, er_sem, rs_sem, rr_sem, fs_sem, fr_sem,
):
    node = lax.axis_index("node")
    lane = lax.axis_index("local")
    x, half, spot, core = lane // 16, (lane // 8) % 2, (lane // 2) % 4, lane % 2
    unit = lane % 8

    def place(x_at, half_at, spot_at, core_at):
        return {"node": node, "local": ((x_at * 2 + half_at) * 4 + spot_at) * 2 + core_at}

    z_peer = [{"node": (node + d) % NODES, "local": lane} for d in range(1, 8)]
    x_peer = [place((x + d) % 4, half, spot, core) for d in range(1, 4)]
    y_peer = [place(x, half, (spot + d) % 4, core) for d in range(1, 4)]
    twin = place(x, half, spot, 1 - core)
    far = place(x, 1 - half, spot, core)

    barrier = pltpu.get_barrier_semaphore()
    for peer in z_peer + x_peer + y_peer + [twin, far]:
        pl.semaphore_signal(barrier, inc=1, device_id=peer, device_id_type=MESH)

    sends = []

    def send(src, dst, s_sem, r_sem, peer):
        copy = pltpu.make_async_remote_copy(
            src_ref=src, dst_ref=dst, send_sem=s_sem, recv_sem=r_sem, device_id=peer, device_id_type=MESH
        )
        copy.start()
        sends.append(copy)
        return copy

    loads = [
        pltpu.make_async_copy(src, dst, w_sem.at[i])
        for i, (src, dst) in enumerate([(wg_h, wg), (wu_h, wu), (wd_h, wd)])
    ]
    for load in loads:
        load.start()

    match = (ids[...] & (EXPERTS // NODES - 1)) == 0
    hit = jnp.sum(jnp.where(match, 1.0, 0.0), axis=0, keepdims=True)
    owner = jnp.sum(jnp.where(match, ids[...] // (EXPERTS // NODES), 0), axis=0, keepdims=True)
    share = jnp.sum(jnp.where(match, wts[...], 0.0), axis=0, keepdims=True)
    count = tok.shape[1]
    mine = (lax.broadcasted_iota(jnp.int32, (16, count), 0) == owner) & (hit > 0.0)
    mine = jnp.where(mine, 1.0, 0.0)
    before = lax.broadcasted_iota(jnp.int32, (count, count), 0) < lax.broadcasted_iota(jnp.int32, (count, count), 1)
    rank = nn(mine.astype(BF16), jnp.where(before, 1.0, 0.0).astype(BF16))
    rank = jnp.sum(mine * rank, axis=0, keepdims=True).astype(jnp.int32)
    target = jnp.where(hit > 0.0, owner * CAP + rank, -1)
    chosen = lax.broadcasted_iota(jnp.int32, (NODES * CAP, count), 0) == target
    sel[...] = jnp.where(chosen, 1.0, 0.0).astype(BF16)

    def dispatch(s, source):
        slots = nt(sel[...], source).astype(BF16)
        width = slots.shape[1]
        a_src[s, :, :, 0:width] = slots.reshape(NODES, CAP, width)
        a_dst[s, node] = a_src[s, node]
        return [
            send(a_src.at[s, (node + d) % NODES], a_dst.at[s, node], as_sem.at[s, d - 1], ar_sem.at[s, d - 1], z_peer[d - 1])
            for d in range(1, 8)
        ]

    width = tok.shape[0]

    def landed(s, copies):
        for copy in copies:
            copy.wait_recv()
        block = a_dst[s, :, :, 0:width].reshape(NODES * CAP, width)
        pieces[s, unit] = block.T
        own = pieces.at[s, unit]
        to_twin = send(own, own, gs_sem.at[s, 0], gr_sem.at[s, 0], twin)
        to_line = [send(own, own, bs_sem.at[s, d - 1], br_sem.at[s, d - 1], y_peer[d - 1]) for d in range(1, 4)]
        return to_twin, to_line

    def forward(s, to_line):
        shared = []
        for d in range(1, 4):
            to_line[d - 1].wait_recv()
            block = pieces.at[s, ((spot + 4 - d) % 4) * 2 + core]
            shared.append(send(block, block, gs_sem.at[s, d], gr_sem.at[s, d], twin))
        return shared

    def whole(s):
        return pieces[s].reshape(8 * width, NODES * CAP)

    hid_x = 64

    def scatter(s, first, parts):
        for i, part in enumerate(parts):
            split = part.reshape(4, hid_x, NODES * CAP)
            c_own[:, first + i] = split
            c_src[:, first + i] = split.astype(BF16)
        span = pl.ds(first, len(parts))
        return [
            send(c_src.at[(x + d) % 4, span], c_dst.at[d - 1, span], cs_sem.at[s, d - 1], cr_sem.at[s, d - 1], x_peer[d - 1])
            for d in range(1, 4)
        ]

    def across(s, first, number, copies):
        total = [c_own[x, first + i] for i in range(number)]
        for d in range(1, 4):
            copies[d - 1].wait_recv()
            total = [total[i] + c_dst[d - 1, first + i].astype(F32) for i in range(number)]
        for i in range(number):
            y_src[first + i] = total[i].astype(BF16)
        span = pl.ds(first, number)
        copy = send(y_src.at[span], y_dst.at[span], ys_sem.at[s], yr_sem.at[s], far)
        return total, copy

    def complete(first, total, copy):
        copy.wait_recv()
        return [part + y_dst[first + i].astype(F32) for i, part in enumerate(total)]

    def spread(s, first, values):
        for i, value in enumerate(values):
            rows[x, first + i] = value
        block = rows.at[x, pl.ds(first, len(values))]
        return [send(block, block, ds_sem.at[s, d - 1], dr_sem.at[s, d - 1], x_peer[d - 1]) for d in range(1, 4)]

    def gathered(i):
        return rows[:, i].reshape(4 * hid_x, NODES * CAP)

    def weight_half(weight, which):
        return weight[:, which].reshape(4 * width, weight.shape[3])

    def pair_sum(s, terms):
        def part(which):
            return sum(nn(weight_half(weight, which), value) for weight, value in terms)

        e_src[s] = part(1 - core).reshape(4, width, NODES * CAP).astype(BF16)
        copy = send(e_src.at[s], e_dst.at[s], es_sem.at[s], er_sem.at[s], twin)
        own = part(core).reshape(4, width, NODES * CAP)
        return own, copy

    def line_sum(s, own, copy):
        copy.wait_recv()
        total = own + e_dst[s].astype(F32)
        r_own[s] = total
        r_src[s] = total.astype(BF16)
        return [
            send(r_src.at[s, (spot + d) % 4], r_dst.at[s, d - 1], rs_sem.at[s, d - 1], rr_sem.at[s, d - 1], y_peer[d - 1])
            for d in range(1, 4)
        ]

    def give_back(s, copies):
        total = r_own[s, spot]
        for d in range(1, 4):
            copies[d - 1].wait_recv()
            total = total + r_dst[s, d - 1].astype(F32)
        f_src[s, :, :, 0:width] = total.astype(BF16).T.reshape(NODES, CAP, width)
        f_dst[s, node] = f_src[s, node]
        return [
            send(f_src.at[s, (node + d) % NODES], f_dst.at[s, node], fs_sem.at[s, d - 1], fr_sem.at[s, d - 1], z_peer[d - 1])
            for d in range(1, 8)
        ]

    def combine(s, copies):
        for copy in copies:
            copy.wait_recv()
        block = f_dst[s, :, :, 0:width].reshape(NODES * CAP, width)
        return nn(block.T, sel[...])

    pl.semaphore_wait(barrier, 15)
    a_tok = dispatch(0, tok[...])
    a_grad = dispatch(1, (share * og[...].astype(F32)).astype(BF16))

    for load in loads:
        load.wait()
    hidden_units = wd.shape[0]
    wgt[...] = wg[...].reshape(8 * width, hidden_units).T
    wut[...] = wu[...].reshape(8 * width, hidden_units).T
    wdt[...] = wd[...].T.reshape(4, 2, width, hidden_units)

    twin_tok, line_tok = landed(0, a_tok)
    shared_tok = forward(0, line_tok)
    twin_grad, line_grad = landed(1, a_grad)
    for copy in [twin_tok] + shared_tok:
        copy.wait_recv()
    tokens_t = whole(0)
    c_fwd = scatter(0, 0, [nn(wgt[...], tokens_t), nn(wut[...], tokens_t)])
    sum_fwd, far_fwd = across(0, 0, 2, c_fwd)
    shared_grad = forward(1, line_grad)
    for copy in [twin_grad] + shared_grad:
        copy.wait_recv()
    c_bwd = scatter(1, 2, [nn(wd[...], whole(1))])
    gate_sum, up_sum = complete(0, sum_fwd, far_fwd)
    sig = jax.nn.sigmoid(gate_sum)
    active = gate_sum * sig
    d_fwd = spread(0, 0, [(active * up_sum).astype(BF16)])
    sum_bwd, far_bwd = across(1, 2, 1, c_bwd)
    for copy in d_fwd:
        copy.wait_recv()
    own_fwd, e_fwd = pair_sum(0, [(wdt, gathered(0))])
    (back_sum,) = complete(2, sum_bwd, far_bwd)
    grad_gate = (back_sum * up_sum * sig * (1.0 + gate_sum * (1.0 - sig))).astype(BF16)
    grad_up = (back_sum * active).astype(BF16)
    d_bwd = spread(1, 1, [grad_gate, grad_up])
    r_fwd = line_sum(0, own_fwd, e_fwd)
    dg[...] = nt(gathered(0), whole(1)).astype(BF16)
    stores = [pltpu.make_async_copy(dg, dg_h, o_sem.at[0])]
    stores[0].start()
    for copy in d_bwd:
        copy.wait_recv()
    own_bwd, e_bwd = pair_sum(1, [(wg, gathered(1)), (wu, gathered(2))])
    r_bwd = line_sum(1, own_bwd, e_bwd)
    gg[...] = nt(whole(0), gathered(1)).astype(BF16)
    ug[...] = nt(whole(0), gathered(2)).astype(BF16)
    stores += [pltpu.make_async_copy(gg, gg_h, o_sem.at[1]), pltpu.make_async_copy(ug, ug_h, o_sem.at[2])]
    stores[1].start()
    stores[2].start()
    f_fwd = give_back(0, r_fwd)
    f_bwd = give_back(1, r_bwd)
    lo[...] = (share * combine(0, f_fwd)).astype(BF16)
    ig[...] = combine(1, f_bwd).astype(BF16)
    for copy in sends:
        copy.wait_send()
    for store in stores:
        store.wait()


def on_device(tokens, out_grad, route_ids, route_weights, gate_weight, up_weight, down_weight):
    count, width = tokens.shape
    units, hid = gate_weight.shape[2], gate_weight.shape[3]
    slots = NODES * CAP
    vmem = pl.BlockSpec(memory_space=pltpu.VMEM)
    hbm = pl.BlockSpec(memory_space=pl.ANY)
    dma = pltpu.SemaphoreType.DMA
    shapes = [
        ((4, 2, width, hid), BF16),
        ((4, 2, width, hid), BF16),
        ((hid, units), BF16),
        ((hid, units), BF16),
        ((hid, units), BF16),
        ((4, 2, width, hid), BF16),
        ((slots, count), BF16),
        ((2, NODES, CAP, 128), BF16),
        ((2, NODES, CAP, 128), BF16),
        ((2, 8, width, slots), BF16),
        ((4, 3, hid // 4, slots), F32),
        ((4, 3, hid // 4, slots), BF16),
        ((3, 3, hid // 4, slots), BF16),
        ((3, hid // 4, slots), BF16),
        ((3, hid // 4, slots), BF16),
        ((4, 3, hid // 4, slots), BF16),
        ((2, 4, width, slots), BF16),
        ((2, 4, width, slots), BF16),
        ((2, 4, width, slots), F32),
        ((2, 4, width, slots), BF16),
        ((2, 3, width, slots), BF16),
        ((2, NODES, CAP, 128), BF16),
        ((2, NODES, CAP, 128), BF16),
        ((units, hid), BF16),
        ((units, hid), BF16),
        ((hid, units), BF16),
    ]
    sems = [(3,), (3,), (2, 7), (2, 7), (2, 3), (2, 3), (2, 4), (2, 4), (2, 3), (2, 3), (2,), (2,)]
    sems += [(2, 3), (2, 3), (2,), (2,), (2, 3), (2, 3), (2, 7), (2, 7)]
    lo, ig, gg, ug, dg = pl.pallas_call(
        kernel,
        out_shape=(
            jax.ShapeDtypeStruct((width, count), BF16),
            jax.ShapeDtypeStruct((width, count), BF16),
            jax.ShapeDtypeStruct((units, hid), BF16),
            jax.ShapeDtypeStruct((units, hid), BF16),
            jax.ShapeDtypeStruct((hid, units), BF16),
        ),
        in_specs=[vmem] * 4 + [hbm] * 3,
        out_specs=(vmem, vmem, hbm, hbm, hbm),
        scratch_shapes=[pltpu.VMEM(shape, kind) for shape, kind in shapes] + [dma(shape) for shape in sems],
        compiler_params=pltpu.CompilerParams(collective_id=0, has_side_effects=True, vmem_limit_bytes=40 << 20),
        name="expert_layer",
    )(
        tokens.T,
        out_grad.T,
        route_ids.T,
        route_weights.T,
        gate_weight.reshape(4, 2, width, hid),
        up_weight.reshape(4, 2, width, hid),
        down_weight.reshape(hid, units),
    )
    return (lo.T, ig.T, gg[None, None], ug[None, None], dg[None, None])


def solution(mesh):
    rows = P("node", "local")
    routes = P("node", None)
    blocks = P("node", "local", None, None)
    return jax.shard_map(
        on_device,
        mesh=mesh,
        in_specs=(rows, rows, routes, routes, blocks, blocks, blocks),
        out_specs=(rows, rows, blocks, blocks, blocks),
        check_vma=False,
    )
```

```python
import jax
import jax.numpy as jnp
from jax import lax
from jax.experimental import pallas as pl
from jax.experimental.pallas import tpu as pltpu
from jax.sharding import PartitionSpec as P

EXPERTS = 256
CAP = 32
VMEM_BYTES = 24 << 20
NODES = 8
MESH = pl.DeviceIdType.MESH
BF16 = jnp.bfloat16
F32 = jnp.float32


def nn(left, right):
    return lax.dot_general(left, right, (((1,), (0,)), ((), ())), preferred_element_type=F32)


def nt(left, right):
    return lax.dot_general(left, right, (((1,), (1,)), ((), ())), preferred_element_type=F32)


def slot_numbers(count):
    return lax.broadcasted_iota(jnp.int32, (NODES * CAP, count), 0).astype(F32)


def kernel(
    tok_h, og_h, ids_h, wts_h, wg_h, wu_h, wd_h,
    back, meta, gg, ug, dg,
    tok, og, ids, wts,
    wg, wu, wd, wgt, wut, wdt, sel, a_src, a_dst, pieces,
    c_own, c_src, c_dst, y_src, y_dst, rows, e_src, e_dst, r_own, r_src, r_dst, f_src, f_dst,
    w_sem, as_sem, ar_sem, bs_sem, br_sem, gs_sem, gr_sem, cs_sem, cr_sem, ys_sem, yr_sem,
    ds_sem, dr_sem, es_sem, er_sem, rs_sem, rr_sem, fs_sem, fr_sem,
):
    node = lax.axis_index("node")
    lane = lax.axis_index("local")
    x, half, spot, core = lane // 16, (lane // 8) % 2, (lane // 2) % 4, lane % 2
    unit = lane % 8

    def place(x_at, half_at, spot_at, core_at):
        return {"node": node, "local": ((x_at * 2 + half_at) * 4 + spot_at) * 2 + core_at}

    z_peer = [{"node": (node + d) % NODES, "local": lane} for d in range(1, 8)]
    x_peer = [place((x + d) % 4, half, spot, core) for d in range(1, 4)]
    y_peer = [place(x, half, (spot + d) % 4, core) for d in range(1, 4)]
    twin = place(x, half, spot, 1 - core)
    far = place(x, 1 - half, spot, core)

    barrier = pltpu.get_barrier_semaphore()
    for peer in z_peer + x_peer + y_peer + [twin, far]:
        pl.semaphore_signal(barrier, inc=1, device_id=peer, device_id_type=MESH)

    sends = []

    def send(src, dst, s_sem, r_sem, peer):
        copy = pltpu.make_async_remote_copy(
            src_ref=src, dst_ref=dst, send_sem=s_sem, recv_sem=r_sem, device_id=peer, device_id_type=MESH
        )
        copy.start()
        sends.append(copy)
        return copy

    loads = [
        pltpu.make_async_copy(src, dst, w_sem.at[i])
        for i, (src, dst) in enumerate(
            [(ids_h, ids), (wts_h, wts), (tok_h, tok), (og_h, og), (wg_h, wg), (wu_h, wu), (wd_h, wd)]
        )
    ]
    for load in loads:
        load.start()
    loads[0].wait()
    loads[1].wait()

    match = (ids[...] & (EXPERTS // NODES - 1)) == 0
    hit = jnp.sum(jnp.where(match, 1.0, 0.0), axis=0, keepdims=True)
    owner = jnp.sum(jnp.where(match, ids[...] // (EXPERTS // NODES), 0), axis=0, keepdims=True)
    share = jnp.sum(jnp.where(match, wts[...], 0.0), axis=0, keepdims=True)
    count = tok.shape[1]
    mine = (lax.broadcasted_iota(jnp.int32, (16, count), 0) == owner) & (hit > 0.0)
    mine = jnp.where(mine, 1.0, 0.0)
    before = lax.broadcasted_iota(jnp.int32, (count, count), 0) < lax.broadcasted_iota(jnp.int32, (count, count), 1)
    rank = nn(mine.astype(BF16), jnp.where(before, 1.0, 0.0).astype(BF16))
    rank = jnp.sum(mine * rank, axis=0, keepdims=True).astype(jnp.int32)
    target = jnp.where(hit > 0.0, (owner * CAP + rank).astype(F32), -1.0)
    chosen = slot_numbers(count) == target
    sel[...] = jnp.where(chosen, 1.0, 0.0).astype(BF16)
    meta[0:1] = target
    meta[1:2] = share

    def dispatch(s, source):
        slots = nt(sel[...], source).astype(BF16)
        width = slots.shape[1]
        a_src[s, :, :, 0:width] = slots.reshape(NODES, CAP, width)
        a_dst[s, node] = a_src[s, node]
        return [
            send(a_src.at[s, (node + d) % NODES], a_dst.at[s, node], as_sem.at[s, d - 1], ar_sem.at[s, d - 1], z_peer[d - 1])
            for d in range(1, 8)
        ]

    width = tok.shape[0]

    def landed(s, copies):
        for copy in copies:
            copy.wait_recv()
        block = a_dst[s, :, :, 0:width].reshape(NODES * CAP, width)
        pieces[s, unit] = block.T
        own = pieces.at[s, unit]
        to_twin = send(own, own, gs_sem.at[s, 0], gr_sem.at[s, 0], twin)
        to_line = [send(own, own, bs_sem.at[s, d - 1], br_sem.at[s, d - 1], y_peer[d - 1]) for d in range(1, 4)]
        return to_twin, to_line

    def forward(s, to_line):
        shared = []
        for d in range(1, 4):
            to_line[d - 1].wait_recv()
            block = pieces.at[s, ((spot + 4 - d) % 4) * 2 + core]
            shared.append(send(block, block, gs_sem.at[s, d], gr_sem.at[s, d], twin))
        return shared

    def whole(s):
        return pieces[s].reshape(8 * width, NODES * CAP)

    hid_x = 64

    def scatter(s, first, parts):
        for i, part in enumerate(parts):
            split = part.reshape(4, hid_x, NODES * CAP)
            c_own[:, first + i] = split
            c_src[:, first + i] = split.astype(BF16)
        span = pl.ds(first, len(parts))
        return [
            send(c_src.at[(x + d) % 4, span], c_dst.at[d - 1, span], cs_sem.at[s, d - 1], cr_sem.at[s, d - 1], x_peer[d - 1])
            for d in range(1, 4)
        ]

    def across(s, first, number, copies):
        total = [c_own[x, first + i] for i in range(number)]
        for d in range(1, 4):
            copies[d - 1].wait_recv()
            total = [total[i] + c_dst[d - 1, first + i].astype(F32) for i in range(number)]
        for i in range(number):
            y_src[first + i] = total[i].astype(BF16)
        span = pl.ds(first, number)
        copy = send(y_src.at[span], y_dst.at[span], ys_sem.at[s], yr_sem.at[s], far)
        return total, copy

    def complete(first, total, copy):
        copy.wait_recv()
        return [part + y_dst[first + i].astype(F32) for i, part in enumerate(total)]

    def spread(s, first, values):
        for i, value in enumerate(values):
            rows[x, first + i] = value
        block = rows.at[x, pl.ds(first, len(values))]
        return [send(block, block, ds_sem.at[s, d - 1], dr_sem.at[s, d - 1], x_peer[d - 1]) for d in range(1, 4)]

    def gathered(i):
        return rows[:, i].reshape(4 * hid_x, NODES * CAP)

    def weight_half(weight, which):
        return weight[:, which].reshape(4 * width, weight.shape[3])

    def pair_sum(s, terms):
        def part(which):
            return sum(nn(weight_half(weight, which), value) for weight, value in terms)

        e_src[s] = part(1 - core).reshape(4, width, NODES * CAP).astype(BF16)
        copy = send(e_src.at[s], e_dst.at[s], es_sem.at[s], er_sem.at[s], twin)
        own = part(core).reshape(4, width, NODES * CAP)
        return own, copy

    def line_sum(s, own, copy):
        copy.wait_recv()
        total = own + e_dst[s].astype(F32)
        r_own[s] = total
        r_src[s] = total.astype(BF16)
        return [
            send(r_src.at[s, (spot + d) % 4], r_dst.at[s, d - 1], rs_sem.at[s, d - 1], rr_sem.at[s, d - 1], y_peer[d - 1])
            for d in range(1, 4)
        ]

    def give_back(s, copies):
        total = r_own[s, spot]
        for d in range(1, 4):
            copies[d - 1].wait_recv()
            total = total + r_dst[s, d - 1].astype(F32)
        f_src[s, :, :, 0:width] = total.astype(BF16).T.reshape(NODES, CAP, width)
        f_dst[s, node] = f_src[s, node]
        return [
            send(f_src.at[s, (node + d) % NODES], f_dst.at[s, node], fs_sem.at[s, d - 1], fr_sem.at[s, d - 1], z_peer[d - 1])
            for d in range(1, 8)
        ]

    pl.semaphore_wait(barrier, 15)
    loads[2].wait()
    a_tok = dispatch(0, tok[...])
    loads[3].wait()
    a_grad = dispatch(1, (share * og[...].astype(F32)).astype(BF16))

    for load in loads[4:]:
        load.wait()
    hidden_units = wd.shape[0]
    wgt[...] = wg[...].reshape(8 * width, hidden_units).T
    wut[...] = wu[...].reshape(8 * width, hidden_units).T
    wdt[...] = wd[...].T.reshape(4, 2, width, hidden_units)

    twin_tok, line_tok = landed(0, a_tok)
    shared_tok = forward(0, line_tok)
    twin_grad, line_grad = landed(1, a_grad)
    for copy in [twin_tok] + shared_tok:
        copy.wait_recv()
    tokens_t = whole(0)
    c_fwd = scatter(0, 0, [nn(wgt[...], tokens_t), nn(wut[...], tokens_t)])
    sum_fwd, far_fwd = across(0, 0, 2, c_fwd)
    shared_grad = forward(1, line_grad)
    for copy in [twin_grad] + shared_grad:
        copy.wait_recv()
    c_bwd = scatter(1, 2, [nn(wd[...], whole(1))])
    gate_sum, up_sum = complete(0, sum_fwd, far_fwd)
    sig = jax.nn.sigmoid(gate_sum)
    active = gate_sum * sig
    d_fwd = spread(0, 0, [(active * up_sum).astype(BF16)])
    sum_bwd, far_bwd = across(1, 2, 1, c_bwd)
    for copy in d_fwd:
        copy.wait_recv()
    own_fwd, e_fwd = pair_sum(0, [(wdt, gathered(0))])
    (back_sum,) = complete(2, sum_bwd, far_bwd)
    grad_gate = (back_sum * up_sum * sig * (1.0 + gate_sum * (1.0 - sig))).astype(BF16)
    grad_up = (back_sum * active).astype(BF16)
    d_bwd = spread(1, 1, [grad_gate, grad_up])
    r_fwd = line_sum(0, own_fwd, e_fwd)
    dg[...] = nt(gathered(0), whole(1)).astype(BF16)
    for copy in d_bwd:
        copy.wait_recv()
    own_bwd, e_bwd = pair_sum(1, [(wg, gathered(1)), (wu, gathered(2))])
    r_bwd = line_sum(1, own_bwd, e_bwd)
    gg[...] = nt(whole(0), gathered(1)).astype(BF16)
    ug[...] = nt(whole(0), gathered(2)).astype(BF16)
    f_fwd = give_back(0, r_fwd)
    f_bwd = give_back(1, r_bwd)
    for copy in f_fwd + f_bwd:
        copy.wait_recv()
    back[...] = f_dst[...]
    for copy in sends:
        copy.wait_send()


def finish(back, meta, gg, ug, dg, lo, ig, gg_h, ug_h, dg_h, sems):
    copies = [
        pltpu.make_async_copy(src, dst, sems.at[i]) for i, (src, dst) in enumerate([(gg, gg_h), (ug, ug_h), (dg, dg_h)])
    ]
    for copy in copies:
        copy.start()
    width, count = lo.shape
    sel = jnp.where(slot_numbers(count) == meta[0:1], 1.0, 0.0).astype(BF16)
    lo[...] = (meta[1:2] * nn(back[0, :, :, 0:width].reshape(NODES * CAP, width).T, sel)).astype(BF16)
    ig[...] = nn(back[1, :, :, 0:width].reshape(NODES * CAP, width).T, sel).astype(BF16)
    for copy in copies:
        copy.wait()


def on_device(tokens, out_grad, route_ids, route_weights, gate_weight, up_weight, down_weight):
    count, width = tokens.shape
    units, hid = gate_weight.shape[2], gate_weight.shape[3]
    slots = NODES * CAP
    vmem = pl.BlockSpec(memory_space=pltpu.VMEM)
    hbm = pl.BlockSpec(memory_space=pltpu.HBM)
    dma = pltpu.SemaphoreType.DMA
    shapes = [
        ((width, count), BF16),
        ((width, count), BF16),
        (route_ids.shape[::-1], jnp.int32),
        (route_ids.shape[::-1], F32),
        ((4, 2, width, hid), BF16),
        ((4, 2, width, hid), BF16),
        ((hid, units), BF16),
        ((hid, units), BF16),
        ((hid, units), BF16),
        ((4, 2, width, hid), BF16),
        ((slots, count), BF16),
        ((2, NODES, CAP, 128), BF16),
        ((2, NODES, CAP, 128), BF16),
        ((2, 8, width, slots), BF16),
        ((4, 3, hid // 4, slots), F32),
        ((4, 3, hid // 4, slots), BF16),
        ((3, 3, hid // 4, slots), BF16),
        ((3, hid // 4, slots), BF16),
        ((3, hid // 4, slots), BF16),
        ((4, 3, hid // 4, slots), BF16),
        ((2, 4, width, slots), BF16),
        ((2, 4, width, slots), BF16),
        ((2, 4, width, slots), F32),
        ((2, 4, width, slots), BF16),
        ((2, 3, width, slots), BF16),
        ((2, NODES, CAP, 128), BF16),
        ((2, NODES, CAP, 128), BF16),
    ]
    sems = [(7,), (2, 7), (2, 7), (2, 3), (2, 3), (2, 4), (2, 4), (2, 3), (2, 3), (2,), (2,)]
    sems += [(2, 3), (2, 3), (2,), (2,), (2, 3), (2, 3), (2, 7), (2, 7)]
    operands = (
        tokens.T,
        out_grad.T,
        route_ids.T,
        route_weights.T,
        gate_weight.reshape(4, 2, width, hid),
        up_weight.reshape(4, 2, width, hid),
        down_weight.reshape(hid, units),
    )
    back, meta, gg, ug, dg = pl.pallas_call(
        kernel,
        out_shape=(
            jax.ShapeDtypeStruct((2, NODES, CAP, 128), BF16),
            jax.ShapeDtypeStruct((8, count), F32),
            jax.ShapeDtypeStruct((units, hid), BF16),
            jax.ShapeDtypeStruct((units, hid), BF16),
            jax.ShapeDtypeStruct((hid, units), BF16),
        ),
        in_specs=[hbm] * 7,
        out_specs=(vmem,) * 5,
        scratch_shapes=[pltpu.VMEM(shape, kind) for shape, kind in shapes] + [dma(shape) for shape in sems],
        compiler_params=pltpu.CompilerParams(collective_id=0, has_side_effects=True, vmem_limit_bytes=VMEM_BYTES),
        name="expert_layer",
    )(
        *(pltpu.with_memory_space_constraint(array, pltpu.HBM) for array in operands)
    )
    lo, ig, gg, ug, dg = pl.pallas_call(
        finish,
        out_shape=(
            jax.ShapeDtypeStruct((width, count), BF16),
            jax.ShapeDtypeStruct((width, count), BF16),
            jax.ShapeDtypeStruct((units, hid), BF16),
            jax.ShapeDtypeStruct((units, hid), BF16),
            jax.ShapeDtypeStruct((hid, units), BF16),
        ),
        in_specs=[vmem] * 5,
        out_specs=(vmem, vmem, hbm, hbm, hbm),
        scratch_shapes=[dma((3,))],
        compiler_params=pltpu.CompilerParams(vmem_limit_bytes=VMEM_BYTES),
        name="finish",
    )(back, meta, gg, ug, dg)
    return (lo.T, ig.T, gg[None, None], ug[None, None], dg[None, None])


def solution(mesh):
    rows = P("node", "local")
    routes = P("node", None)
    blocks = P("node", "local", None, None)
    return jax.shard_map(
        on_device,
        mesh=mesh,
        in_specs=(rows, rows, routes, routes, blocks, blocks, blocks),
        out_specs=(rows, rows, blocks, blocks, blocks),
        check_vma=False,
    )
```

```python
import jax
import jax.numpy as jnp
from jax import lax
from jax.experimental import pallas as pl
from jax.experimental.pallas import tpu as pltpu
from jax.sharding import PartitionSpec as P

EXPERTS = 256
CAP = 32
VMEM_BYTES = 24 << 20
NODES = 8
MESH = pl.DeviceIdType.MESH
BF16 = jnp.bfloat16
F32 = jnp.float32


def nn(left, right):
    return lax.dot_general(left, right, (((1,), (0,)), ((), ())), preferred_element_type=F32)


def nt(left, right):
    return lax.dot_general(left, right, (((1,), (1,)), ((), ())), preferred_element_type=F32)


def slot_numbers(count):
    return lax.broadcasted_iota(jnp.int32, (NODES * CAP, count), 0).astype(F32)


STEPS = (0, 1, 7, 2, 6, 3, 5, 4)
RUNS = ((0, 4), (4, 8))


def kernel(
    tok_h, og_h, ids_h, wts_h, wg_h, wu_h, wd_h,
    back, meta, gg, ug, dg,
    tok, og, ids, wts, wg, wu, wd, wgt, wut, wdt, far_w, sel, a_src, a_dst, held,
    c_own, c_src, c_dst, y_own, y_src, y_dst, act, rows, r_own, r_src, r_dst, f_src, f_dst,
    w_sem, as_sem, ar_sem, bs_sem, br_sem, gs_sem, gr_sem, cs_sem, cr_sem, ys_sem, yr_sem,
    ds_sem, dr_sem, es_sem, er_sem, rs_sem, rr_sem, fs_sem, fr_sem, xs_sem, xr_sem,
):
    node = lax.axis_index("node")
    lane = lax.axis_index("local")
    x, half, spot, core = lane // 16, (lane // 8) % 2, (lane // 2) % 4, lane % 2
    unit = lane % 8

    def place(x_at, half_at, spot_at, core_at):
        return {"node": node, "local": ((x_at * 2 + half_at) * 4 + spot_at) * 2 + core_at}

    def after(j):
        return (node + STEPS[j]) % NODES

    def ahead(j):
        return (node + NODES - STEPS[j]) % NODES

    z_peer = [{"node": (node + d) % NODES, "local": lane} for d in range(1, 8)]
    x_peer = [place((x + d) % 4, half, spot, core) for d in range(1, 4)]
    y_peer = [place(x, half, (spot + d) % 4, core) for d in range(1, 4)]
    twin = place(x, half, spot, 1 - core)
    far = place(x, 1 - half, spot, core)

    barrier = pltpu.get_barrier_semaphore()
    for peer in z_peer + x_peer + y_peer + [twin, far]:
        pl.semaphore_signal(barrier, inc=1, device_id=peer, device_id_type=MESH)

    sends = []

    def send(src, dst, s_sem, r_sem, peer):
        copy = pltpu.make_async_remote_copy(
            src_ref=src, dst_ref=dst, send_sem=s_sem, recv_sem=r_sem, device_id=peer, device_id_type=MESH
        )
        copy.start()
        sends.append(copy)
        return copy

    width = tok_h.shape[0]
    units, hid = 8 * width, wd.shape[0]
    slots = NODES * CAP
    run = slots // 2
    count = tok.shape[1]
    loads = [
        pltpu.make_async_copy(src, dst, w_sem.at[i])
        for i, (src, dst) in enumerate(
            [
                (ids_h, ids),
                (wts_h, wts),
                (tok_h, tok.at[pl.ds(0, width)]),
                (og_h, og.at[pl.ds(0, width)]),
                (wg_h.at[:, 0], wg.at[0]),
                (wg_h.at[:, 1], wg.at[1]),
                (wu_h.at[:, 0], wu.at[0]),
                (wu_h.at[:, 1], wu.at[1]),
                (wd_h, wd),
            ]
        )
    ]
    for load in loads:
        load.start()
    tok[pl.ds(width, 128 - width)] = jnp.zeros((128 - width, count), BF16)
    og[pl.ds(width, 128 - width)] = jnp.zeros((128 - width, count), BF16)
    before = lax.broadcasted_iota(jnp.int32, (count, count), 0) < lax.broadcasted_iota(jnp.int32, (count, count), 1)
    before = jnp.where(before, 1.0, 0.0).astype(BF16)
    loads[0].wait()

    match = (ids[...] & (EXPERTS // NODES - 1)) == 0
    hit = jnp.sum(jnp.where(match, 1.0, 0.0), axis=0, keepdims=True)
    owner = jnp.sum(jnp.where(match, ids[...] // (EXPERTS // NODES), 0), axis=0, keepdims=True)
    mine = (lax.broadcasted_iota(jnp.int32, (16, count), 0) == owner) & (hit > 0.0)
    mine = jnp.where(mine, 1.0, 0.0)
    rank = nn(mine.astype(BF16), before)
    rank = jnp.sum(mine * rank, axis=0, keepdims=True)
    target = jnp.where(hit > 0.0, (owner * CAP).astype(F32) + rank, -1.0)
    sel[...] = jnp.where(slot_numbers(count) == target, 1.0, 0.0).astype(BF16)

    def dispatch(s, source):
        a_src[s] = nt(sel[...], source).astype(BF16).reshape(NODES, CAP, 128)
        copies = [None]
        for j in range(1, 8):
            peer = {"node": ahead(j), "local": lane}
            copies.append(send(a_src.at[s, ahead(j)], a_dst.at[s, j], as_sem.at[s, j - 1], ar_sem.at[s, j - 1], peer))
        a_dst[s, 0] = a_src[s, node]
        return copies

    def gather(s, h, copies):
        low, high = RUNS[h]
        for copy in copies[max(low, 1) : high]:
            copy.wait_recv()
        held[s, h, core, spot] = a_dst[s, low:high].reshape(run, 128).T[0:width]
        own = held.at[s, h, core, spot]
        to_line = [send(own, own, bs_sem.at[s, h, d - 1], br_sem.at[s, h, d - 1], y_peer[d - 1]) for d in range(1, 4)]
        to_twin = send(own, own, gs_sem.at[s, h, 0], gr_sem.at[s, h, 0], twin)
        return to_twin, to_line

    def forward(s, h, state):
        to_twin, to_line = state
        shared = [to_twin]
        for d in range(1, 4):
            to_line[d - 1].wait_recv()
            block = held.at[s, h, core, (spot + 4 - d) % 4]
            shared.append(send(block, block, gs_sem.at[s, h, d], gr_sem.at[s, h, d], twin))
        return shared

    def in_order(blocks):
        return jnp.concatenate([blocks(k, p) for p in range(4) for k in range(2)], axis=0)

    def whole(s, h):
        return in_order(lambda k, p: held[s, h, k, p])

    def all_rows(part):
        return jnp.concatenate([part(h) for h in range(2)], axis=1)

    def scatter(s, h, first, parts):
        for i, part in enumerate(parts):
            split = part.reshape(4, hid // 4, run)
            c_own[h, :, first + i] = split
            c_src[h, :, first + i] = split.astype(BF16)
        span = pl.ds(first, len(parts))
        return [
            send(
                c_src.at[h, (x + d) % 4, span],
                c_dst.at[h, d - 1, span],
                cs_sem.at[s, h, d - 1],
                cr_sem.at[s, h, d - 1],
                x_peer[d - 1],
            )
            for d in range(1, 4)
        ]

    def across(s, h, first, number, copies):
        span = slice(first, first + number)
        total = c_own[h, x, span]
        for d in range(1, 4):
            copies[d - 1].wait_recv()
            total = total + c_dst[h, d - 1, span].astype(F32)
        y_src[h, span] = total.astype(BF16)
        y_own[h, span] = total
        span = pl.ds(first, number)
        return send(y_src.at[h, span], y_dst.at[h, span], ys_sem.at[s, h], yr_sem.at[s, h], far)

    def complete(h, first, number, copy):
        copy.wait_recv()
        return [y_own[h, first + i] + y_dst[h, first + i].astype(F32) for i in range(number)]

    def spread(s, h, first, values):
        for i, value in enumerate(values):
            rows[h, core, x, first + i] = value
        span = pl.ds(first, len(values))
        block = rows.at[h, core, x, span]
        out = [send(block, block, ds_sem.at[s, h, d - 1], dr_sem.at[s, h, d - 1], x_peer[d - 1]) for d in range(1, 4)]
        shared = [send(block, block, es_sem.at[s, h, 0], er_sem.at[s, h, 0], twin)]
        return span, out, shared

    def pass_on(s, h, state):
        span, out, shared = state
        for d in range(1, 4):
            out[d - 1].wait_recv()
            block = rows.at[h, core, (x + 4 - d) % 4, span]
            shared.append(send(block, block, es_sem.at[s, h, d], er_sem.at[s, h, d], twin))
        return shared

    def gathered(h, which, i):
        return rows[h, which, :, i].reshape(hid, run)

    def line_sum(s, h, terms, shared):
        total = sum(nn(own[core].reshape(4 * width, hid), gathered(h, core, i)) for i, own, _ in terms)
        for copy in shared:
            copy.wait_recv()
        total += sum(nn(far_w[f].reshape(4 * width, hid), gathered(h, 1 - core, i)) for i, _, f in terms)
        total = total.reshape(4, width, run)
        r_src[s, h] = total.astype(BF16)
        r_own[s, h] = total
        return [
            send(
                r_src.at[s, h, (spot + d) % 4],
                r_dst.at[s, h, d - 1],
                rs_sem.at[s, h, d - 1],
                rr_sem.at[s, h, d - 1],
                y_peer[d - 1],
            )
            for d in range(1, 4)
        ]

    def give_back(s, h, copies):
        low, high = RUNS[h]
        total = r_own[s, h, spot]
        for d in range(1, 4):
            copies[d - 1].wait_recv()
            total = total + r_dst[s, h, d - 1].astype(F32)
        f_src[s, low:high, :, 0:width] = total.astype(BF16).T.reshape(high - low, CAP, width)
        out = []
        for j in range(max(low, 1), high):
            peer = {"node": after(j), "local": lane}
            out.append(send(f_src.at[s, j], f_dst.at[s, node], fs_sem.at[s, j - 1], fr_sem.at[s, j - 1], peer))
        if low == 0:
            f_dst[s, node] = f_src[s, 0]
        return out

    pl.semaphore_wait(barrier, 15)
    loads[2].wait()
    a_tok = dispatch(0, tok[...])
    loads[1].wait()
    share = jnp.sum(jnp.where(match, wts[...], 0.0), axis=0, keepdims=True)
    loads[3].wait()
    a_grad = dispatch(1, (share * og[...].astype(F32)).astype(BF16))
    meta[0:1] = target
    meta[1:2] = share

    for load in loads[4:]:
        load.wait()
    wdt_full = wd[...].T.reshape(4, 2, width, hid)
    wdt[0] = wdt_full[:, 0]
    wdt[1] = wdt_full[:, 1]
    far_copies = [
        send(weight.at[1 - core], far_w.at[i], xs_sem.at[i], xr_sem.at[i], twin) for i, weight in enumerate((wdt, wg, wu))
    ]
    wgt[...] = in_order(lambda k, p: wg[k, p]).T
    wut[...] = in_order(lambda k, p: wu[k, p]).T
    b_tok = [gather(0, h, a_tok) for h in range(2)]
    b_tok = [forward(0, h, b_tok[h]) for h in range(2)]
    b_grad = [gather(1, h, a_grad) for h in range(2)]
    c_fwd, c_bwd, y_fwd, y_bwd, d_fwd, d_bwd = [], [], [], [], [], []
    for h in range(2):
        for copy in b_tok[h]:
            copy.wait_recv()
        tokens = whole(0, h)
        c_fwd.append(scatter(0, h, 0, [nn(wgt[...], tokens), nn(wut[...], tokens)]))

    def activate(h):
        gate_sum, up_sum = complete(h, 0, 2, y_fwd[h])
        sig = jax.nn.sigmoid(gate_sum)
        active = gate_sum * sig
        d_fwd.append(spread(0, h, 0, [(active * up_sum).astype(BF16)]))
        act[h, 0] = up_sum * sig * (1.0 + gate_sum * (1.0 - sig))
        act[h, 1] = active

    def differentiate(h):
        (back_sum,) = complete(h, 2, 1, y_bwd[h])
        d_bwd.append(spread(1, h, 1, [(back_sum * act[h, 0]).astype(BF16), (back_sum * act[h, 1]).astype(BF16)]))

    for h in range(2):
        b_grad[h] = forward(1, h, b_grad[h])
        y_fwd.append(across(0, h, 0, 2, c_fwd[h]))
        for copy in b_grad[h]:
            copy.wait_recv()
        c_bwd.append(scatter(1, h, 2, [nn(wd[...], whole(1, h))]))
    for h in range(2):
        y_bwd.append(across(1, h, 2, 1, c_bwd[h]))
        activate(h)
    for copy in far_copies:
        copy.wait_recv()
    r_fwd, r_bwd, f_fwd, f_bwd = [], [], [], []
    for h in range(2):
        shared = pass_on(0, h, d_fwd[h])
        differentiate(h)
        r_fwd.append(line_sum(0, h, [(0, wdt, 0)], shared))
    for h in range(2):
        shared = pass_on(1, h, d_bwd[h])
        r_bwd.append(line_sum(1, h, [(1, wg, 1), (2, wu, 2)], shared))
    dg[...] = nt(all_rows(lambda h: gathered(h, core, 0)), all_rows(lambda h: whole(1, h))).astype(BF16)
    tokens = all_rows(lambda h: whole(0, h))
    for h in range(2):
        f_fwd += give_back(0, h, r_fwd[h])
    gg[...] = nt(tokens, all_rows(lambda h: gathered(h, core, 1))).astype(BF16)
    ug[...] = nt(tokens, all_rows(lambda h: gathered(h, core, 2))).astype(BF16)
    for h in range(2):
        f_bwd += give_back(1, h, r_bwd[h])
    for copy in f_fwd + f_bwd:
        copy.wait_recv()
    back[...] = f_dst[...]
    for copy in sends:
        copy.wait_send()


def finish(back, meta, gg, ug, dg, lo, ig, gg_h, ug_h, dg_h, sems):
    copies = [
        pltpu.make_async_copy(src, dst, sems.at[i]) for i, (src, dst) in enumerate([(gg, gg_h), (ug, ug_h), (dg, dg_h)])
    ]
    for copy in copies:
        copy.start()
    width, count = lo.shape
    sel = jnp.where(slot_numbers(count) == meta[0:1], 1.0, 0.0).astype(BF16)
    lo[...] = (meta[1:2] * nn(back[0, :, :, 0:width].reshape(NODES * CAP, width).T, sel)).astype(BF16)
    ig[...] = nn(back[1, :, :, 0:width].reshape(NODES * CAP, width).T, sel).astype(BF16)
    for copy in copies:
        copy.wait()


def on_device(tokens, out_grad, route_ids, route_weights, gate_weight, up_weight, down_weight):
    count, width = tokens.shape
    units, hid = gate_weight.shape[2], gate_weight.shape[3]
    slots = NODES * CAP
    run = slots // 2
    vmem = pl.BlockSpec(memory_space=pltpu.VMEM)
    hbm = pl.BlockSpec(memory_space=pltpu.HBM)
    dma = pltpu.SemaphoreType.DMA
    shapes = [
        ((128, count), BF16),
        ((128, count), BF16),
        (route_ids.shape[::-1], jnp.int32),
        (route_ids.shape[::-1], F32),
        ((2, 4, width, hid), BF16),
        ((2, 4, width, hid), BF16),
        ((hid, units), BF16),
        ((hid, units), BF16),
        ((hid, units), BF16),
        ((2, 4, width, hid), BF16),
        ((3, 4, width, hid), BF16),
        ((slots, count), BF16),
        ((2, NODES, CAP, 128), BF16),
        ((2, NODES, CAP, 128), BF16),
        ((2, 2, 2, 4, width, run), BF16),
        ((2, 4, 3, hid // 4, run), F32),
        ((2, 4, 3, hid // 4, run), BF16),
        ((2, 3, 3, hid // 4, run), BF16),
        ((2, 3, hid // 4, run), F32),
        ((2, 3, hid // 4, run), BF16),
        ((2, 3, hid // 4, run), BF16),
        ((2, 2, hid // 4, run), F32),
        ((2, 2, 4, 3, hid // 4, run), BF16),
        ((2, 2, 4, width, run), F32),
        ((2, 2, 4, width, run), BF16),
        ((2, 2, 3, width, run), BF16),
        ((2, NODES, CAP, 128), BF16),
        ((2, NODES, CAP, 128), BF16),
    ]
    sems = [(9,), (2, 7), (2, 7), (2, 2, 3), (2, 2, 3), (2, 2, 4), (2, 2, 4), (2, 2, 3), (2, 2, 3), (2, 2), (2, 2)]
    sems += [(2, 2, 3), (2, 2, 3), (2, 2, 4), (2, 2, 4), (2, 2, 3), (2, 2, 3), (2, 7), (2, 7), (3,), (3,)]
    operands = (
        tokens.T,
        out_grad.T,
        route_ids.T,
        route_weights.T,
        gate_weight.reshape(4, 2, width, hid),
        up_weight.reshape(4, 2, width, hid),
        down_weight.reshape(hid, units),
    )
    back, meta, gg, ug, dg = pl.pallas_call(
        kernel,
        out_shape=(
            jax.ShapeDtypeStruct((2, NODES, CAP, 128), BF16),
            jax.ShapeDtypeStruct((8, count), F32),
            jax.ShapeDtypeStruct((units, hid), BF16),
            jax.ShapeDtypeStruct((units, hid), BF16),
            jax.ShapeDtypeStruct((hid, units), BF16),
        ),
        in_specs=[hbm] * 7,
        out_specs=(vmem,) * 5,
        scratch_shapes=[pltpu.VMEM(shape, kind) for shape, kind in shapes] + [dma(shape) for shape in sems],
        compiler_params=pltpu.CompilerParams(collective_id=0, has_side_effects=True, vmem_limit_bytes=VMEM_BYTES),
        name="expert_layer",
    )(
        *(pltpu.with_memory_space_constraint(array, pltpu.HBM) for array in operands)
    )
    lo, ig, gg, ug, dg = pl.pallas_call(
        finish,
        out_shape=(
            jax.ShapeDtypeStruct((width, count), BF16),
            jax.ShapeDtypeStruct((width, count), BF16),
            jax.ShapeDtypeStruct((units, hid), BF16),
            jax.ShapeDtypeStruct((units, hid), BF16),
            jax.ShapeDtypeStruct((hid, units), BF16),
        ),
        in_specs=[vmem] * 5,
        out_specs=(vmem, vmem, hbm, hbm, hbm),
        scratch_shapes=[dma((3,))],
        compiler_params=pltpu.CompilerParams(vmem_limit_bytes=VMEM_BYTES),
        name="finish",
    )(back, meta, gg, ug, dg)
    return (lo.T, ig.T, gg[None, None], ug[None, None], dg[None, None])


def solution(mesh):
    rows = P("node", "local")
    routes = P("node", None)
    blocks = P("node", "local", None, None)
    return jax.shard_map(
        on_device,
        mesh=mesh,
        in_specs=(rows, rows, routes, routes, blocks, blocks, blocks),
        out_specs=(rows, rows, blocks, blocks, blocks),
        check_vma=False,
    )
```

```python
import jax
import jax.numpy as jnp
from jax import lax
from jax.experimental import pallas as pl
from jax.experimental.pallas import tpu as pltpu
from jax.sharding import PartitionSpec as P

EXPERTS = 256
CAP = 32
VMEM_BYTES = 24 << 20
NODES = 8
MESH = pl.DeviceIdType.MESH
BF16 = jnp.bfloat16
F32 = jnp.float32


def nn(left, right):
    return lax.dot_general(left, right, (((1,), (0,)), ((), ())), preferred_element_type=F32)


def nt(left, right):
    return lax.dot_general(left, right, (((1,), (1,)), ((), ())), preferred_element_type=F32)


def slot_numbers(count):
    return lax.broadcasted_iota(jnp.int32, (NODES * CAP, count), 0).astype(F32)


STEPS = (0, 1, 7, 2, 6, 3, 5, 4)
RUNS = ((0, 4), (4, 8))


def kernel(
    tok_h, og_h, ids_h, wts_h, wg_h, wu_h, wd_h,
    lo, ig, gg, ug, dg,
    tok, og, ids, wts, wg, wu, wd, wgt, wut, wdt, far_w, sel, a_src, a_dst, held,
    c_own, c_src, c_dst, y_own, y_src, y_dst, act, rows, r_own, r_src, r_dst, f_src, f_dst,
    w_sem, as_sem, ar_sem, bs_sem, br_sem, gs_sem, gr_sem, cs_sem, cr_sem, ys_sem, yr_sem,
    ds_sem, dr_sem, es_sem, er_sem, rs_sem, rr_sem, fs_sem, fr_sem, xs_sem, xr_sem,
):
    node = lax.axis_index("node")
    lane = lax.axis_index("local")
    x, half, spot, core = lane // 16, (lane // 8) % 2, (lane // 2) % 4, lane % 2
    unit = lane % 8

    def place(x_at, half_at, spot_at, core_at):
        return {"node": node, "local": ((x_at * 2 + half_at) * 4 + spot_at) * 2 + core_at}

    def after(j):
        return (node + STEPS[j]) % NODES

    def ahead(j):
        return (node + NODES - STEPS[j]) % NODES

    z_peer = [{"node": (node + d) % NODES, "local": lane} for d in range(1, 8)]
    x_peer = [place((x + d) % 4, half, spot, core) for d in range(1, 4)]
    y_peer = [place(x, half, (spot + d) % 4, core) for d in range(1, 4)]
    x_twin = [place((x + d) % 4, half, spot, 1 - core) for d in range(1, 4)]
    twin = place(x, half, spot, 1 - core)
    far = place(x, 1 - half, spot, core)

    barrier = pltpu.get_barrier_semaphore()
    for peer in z_peer + x_peer + x_twin + y_peer + [twin, far]:
        pl.semaphore_signal(barrier, inc=1, device_id=peer, device_id_type=MESH)

    sends = []

    def send(src, dst, s_sem, r_sem, peer):
        copy = pltpu.make_async_remote_copy(
            src_ref=src, dst_ref=dst, send_sem=s_sem, recv_sem=r_sem, device_id=peer, device_id_type=MESH
        )
        copy.start()
        sends.append(copy)
        return copy

    width = tok_h.shape[0]
    units, hid = 8 * width, wd.shape[0]
    slots = NODES * CAP
    run = slots // 2
    count = tok.shape[1]
    loads = [
        pltpu.make_async_copy(src, dst, w_sem.at[i])
        for i, (src, dst) in enumerate(
            [
                (ids_h, ids),
                (wts_h, wts),
                (tok_h, tok.at[pl.ds(0, width)]),
                (og_h, og.at[pl.ds(0, width)]),
                (wg_h.at[:, 0], wg.at[0]),
                (wg_h.at[:, 1], wg.at[1]),
                (wu_h.at[:, 0], wu.at[0]),
                (wu_h.at[:, 1], wu.at[1]),
                (wd_h, wd),
            ]
        )
    ]
    for load in loads:
        load.start()
    tok[pl.ds(width, 128 - width)] = jnp.zeros((128 - width, count), BF16)
    og[pl.ds(width, 128 - width)] = jnp.zeros((128 - width, count), BF16)
    before = lax.broadcasted_iota(jnp.int32, (128, 128), 0) < lax.broadcasted_iota(jnp.int32, (128, 128), 1)
    before = jnp.where(before, 1.0, 0.0).astype(BF16)
    loads[0].wait()

    match = (ids[...] & (EXPERTS // NODES - 1)) == 0
    hit = jnp.sum(jnp.where(match, 1.0, 0.0), axis=0, keepdims=True)
    owner = jnp.sum(jnp.where(match, ids[...] // (EXPERTS // NODES), 0), axis=0, keepdims=True)
    mine = (lax.broadcasted_iota(jnp.int32, (16, count), 0) == owner) & (hit > 0.0)
    mine = jnp.where(mine, 1.0, 0.0)
    blocks = [mine[:, low : low + 128] for low in range(0, count, 128)]
    within = nn(jnp.concatenate(blocks, axis=0).astype(BF16), before)
    rank, passed = [], jnp.zeros((16, 1), F32)
    for b, block in enumerate(blocks):
        rank.append(jnp.sum(block * (within[16 * b : 16 * b + 16] + passed), axis=0, keepdims=True))
        passed = passed + jnp.sum(block, axis=1, keepdims=True)
    rank = jnp.concatenate(rank, axis=1)
    target = jnp.where(hit > 0.0, (owner * CAP).astype(F32) + rank, -1.0)
    sel[...] = jnp.where(slot_numbers(count) == target, 1.0, 0.0).astype(BF16)

    def dispatch(s, source):
        a_src[s] = nt(sel[...], source).astype(BF16).reshape(NODES, CAP, 128)
        copies = [None]
        for j in range(1, 8):
            peer = {"node": ahead(j), "local": lane}
            copies.append(send(a_src.at[s, ahead(j)], a_dst.at[s, j], as_sem.at[s, j - 1], ar_sem.at[s, j - 1], peer))
        a_dst[s, 0] = a_src[s, node]
        return copies

    def gather(s, h, copies):
        low, high = RUNS[h]
        for copy in copies[max(low, 1) : high]:
            copy.wait_recv()
        held[s, h, core, spot] = a_dst[s, low:high].reshape(run, 128).T[0:width]
        own = held.at[s, h, core, spot]
        to_line = [send(own, own, bs_sem.at[s, h, d - 1], br_sem.at[s, h, d - 1], y_peer[d - 1]) for d in range(1, 4)]
        to_twin = send(own, own, gs_sem.at[s, h, 0], gr_sem.at[s, h, 0], twin)
        return to_twin, to_line

    def forward(s, h, state):
        to_twin, to_line = state
        shared = [to_twin]
        for d in range(1, 4):
            to_line[d - 1].wait_recv()
            block = held.at[s, h, core, (spot + 4 - d) % 4]
            shared.append(send(block, block, gs_sem.at[s, h, d], gr_sem.at[s, h, d], twin))
        return shared

    def in_order(blocks):
        return jnp.concatenate([blocks(k, p) for p in range(4) for k in range(2)], axis=0)

    def whole(s, h):
        return in_order(lambda k, p: held[s, h, k, p])

    def all_rows(part):
        return jnp.concatenate([part(h) for h in range(2)], axis=1)

    def scatter(s, h, first, parts):
        for i, part in enumerate(parts):
            split = part.reshape(4, hid // 4, run)
            c_own[h, :, first + i] = split
            c_src[h, :, first + i] = split.astype(BF16)
        span = pl.ds(first, len(parts))
        return [
            send(
                c_src.at[h, (x + d) % 4, span],
                c_dst.at[h, d - 1, span],
                cs_sem.at[s, h, d - 1],
                cr_sem.at[s, h, d - 1],
                x_peer[d - 1],
            )
            for d in range(1, 4)
        ]

    def across(s, h, first, number, copies):
        span = slice(first, first + number)
        total = c_own[h, x, span]
        for d in range(1, 4):
            copies[d - 1].wait_recv()
            total = total + c_dst[h, d - 1, span].astype(F32)
        y_src[h, span] = total.astype(BF16)
        y_own[h, span] = total
        span = pl.ds(first, number)
        return send(y_src.at[h, span], y_dst.at[h, span], ys_sem.at[s, h], yr_sem.at[s, h], far)

    def complete(h, first, number, copy):
        copy.wait_recv()
        return [y_own[h, first + i] + y_dst[h, first + i].astype(F32) for i in range(number)]

    def spread(s, h, first, values):
        for i, value in enumerate(values):
            rows[h, core, x, first + i] = value
        span = pl.ds(first, len(values))
        block = rows.at[h, core, x, span]
        out = [send(block, block, ds_sem.at[s, h, d - 1], dr_sem.at[s, h, d - 1], x_peer[d - 1]) for d in range(1, 4)]
        shared = [send(block, block, es_sem.at[s, h, 0], er_sem.at[s, h, 0], twin)]
        if s == 0:
            shared += [send(block, block, es_sem.at[s, h, d], er_sem.at[s, h, d], x_twin[d - 1]) for d in range(1, 4)]
        return span, out, shared

    def pass_on(s, h, state):
        span, out, shared = state
        for d in range(1, 4):
            out[d - 1].wait_recv()
            if s == 1:
                block = rows.at[h, core, (x + 4 - d) % 4, span]
                shared.append(send(block, block, es_sem.at[s, h, d], er_sem.at[s, h, d], twin))
        return shared

    def gathered(h, which, i):
        return rows[h, which, :, i].reshape(hid, run)

    def line_sum(s, h, terms, shared):
        total = sum(nn(own[core].reshape(4 * width, hid), gathered(h, core, i)) for i, own, _ in terms)
        for copy in shared:
            copy.wait_recv()
        total += sum(nn(far_w[f].reshape(4 * width, hid), gathered(h, 1 - core, i)) for i, _, f in terms)
        total = total.reshape(4, width, run)
        r_src[s, h] = total.astype(BF16)
        r_own[s, h] = total
        return [
            send(
                r_src.at[s, h, (spot + d) % 4],
                r_dst.at[s, h, d - 1],
                rs_sem.at[s, h, d - 1],
                rr_sem.at[s, h, d - 1],
                y_peer[d - 1],
            )
            for d in range(1, 4)
        ]

    def give_back(s, h, copies):
        low, high = RUNS[h]
        total = r_own[s, h, spot]
        for d in range(1, 4):
            copies[d - 1].wait_recv()
            total = total + r_dst[s, h, d - 1].astype(F32)
        f_src[s, low:high, :, 0:width] = total.astype(BF16).T.reshape(high - low, CAP, width)
        out = []
        for j in range(max(low, 1), high):
            peer = {"node": after(j), "local": lane}
            out.append(send(f_src.at[s, j], f_dst.at[s, node], fs_sem.at[s, j - 1], fr_sem.at[s, j - 1], peer))
        if low == 0:
            f_dst[s, node] = f_src[s, 0]
        return out

    pl.semaphore_wait(barrier, 18)
    loads[2].wait()
    a_tok = dispatch(0, tok[...])
    loads[1].wait()
    share = jnp.sum(jnp.where(match, wts[...], 0.0), axis=0, keepdims=True)
    loads[3].wait()
    a_grad = dispatch(1, (share * og[...].astype(F32)).astype(BF16))

    for load in loads[4:]:
        load.wait()
    wdt_full = wd[...].T.reshape(4, 2, width, hid)
    wdt[0] = wdt_full[:, 0]
    wdt[1] = wdt_full[:, 1]
    far_copies = [
        send(weight.at[1 - core], far_w.at[i], xs_sem.at[i], xr_sem.at[i], twin) for i, weight in enumerate((wdt, wg, wu))
    ]
    wgt[...] = in_order(lambda k, p: wg[k, p]).T
    wut[...] = in_order(lambda k, p: wu[k, p]).T
    b_tok = [gather(0, h, a_tok) for h in range(2)]
    b_tok = [forward(0, h, b_tok[h]) for h in range(2)]
    b_grad = [gather(1, h, a_grad) for h in range(2)]
    c_fwd, c_bwd, y_fwd, y_bwd, d_fwd, d_bwd = [], [], [], [], [], []
    for h in range(2):
        for copy in b_tok[h]:
            copy.wait_recv()
        tokens = whole(0, h)
        c_fwd.append(scatter(0, h, 0, [nn(wgt[...], tokens), nn(wut[...], tokens)]))

    def activate(h):
        gate_sum, up_sum = complete(h, 0, 2, y_fwd[h])
        sig = jax.nn.sigmoid(gate_sum)
        active = gate_sum * sig
        d_fwd.append(spread(0, h, 0, [(active * up_sum).astype(BF16)]))
        act[h, 0] = up_sum * sig * (1.0 + gate_sum * (1.0 - sig))
        act[h, 1] = active

    def differentiate(h):
        (back_sum,) = complete(h, 2, 1, y_bwd[h])
        d_bwd.append(spread(1, h, 1, [(back_sum * act[h, 0]).astype(BF16), (back_sum * act[h, 1]).astype(BF16)]))

    for h in range(2):
        b_grad[h] = forward(1, h, b_grad[h])
        y_fwd.append(across(0, h, 0, 2, c_fwd[h]))
        for copy in b_grad[h]:
            copy.wait_recv()
        c_bwd.append(scatter(1, h, 2, [nn(wd[...], whole(1, h))]))
    for h in range(2):
        y_bwd.append(across(1, h, 2, 1, c_bwd[h]))
        activate(h)
    for copy in far_copies:
        copy.wait_recv()
    r_fwd, r_bwd, f_fwd, f_bwd = [], [], [], []
    for h in range(2):
        shared = pass_on(0, h, d_fwd[h])
        differentiate(h)
        r_fwd.append(line_sum(0, h, [(0, wdt, 0)], shared))
    for h in range(2):
        shared = pass_on(1, h, d_bwd[h])
        r_bwd.append(line_sum(1, h, [(1, wg, 1), (2, wu, 2)], shared))
    dg[...] = nt(all_rows(lambda h: gathered(h, core, 0)), all_rows(lambda h: whole(1, h))).astype(BF16)
    tokens = all_rows(lambda h: whole(0, h))
    for h in range(2):
        f_fwd += give_back(0, h, r_fwd[h])
    gg[...] = nt(tokens, all_rows(lambda h: gathered(h, core, 1))).astype(BF16)
    ug[...] = nt(tokens, all_rows(lambda h: gathered(h, core, 2))).astype(BF16)
    for h in range(2):
        f_bwd += give_back(1, h, r_bwd[h])

    def combine(s, copies):
        for copy in copies:
            copy.wait_recv()
        return nn(f_dst[s, :, :, 0:width].reshape(slots, width).T, sel[...])

    lo[...] = (share * combine(0, f_fwd)).astype(BF16)
    ig[...] = combine(1, f_bwd).astype(BF16)
    for copy in sends:
        copy.wait_send()


def finish(*refs):
    count = len(refs) // 2
    copies = [pltpu.make_async_copy(refs[i], refs[count + i], refs[-1].at[i]) for i in range(count)]
    for copy in copies:
        copy.start()
    for copy in copies:
        copy.wait()


def on_device(tokens, out_grad, route_ids, route_weights, gate_weight, up_weight, down_weight):
    count, width = tokens.shape
    units, hid = gate_weight.shape[2], gate_weight.shape[3]
    slots = NODES * CAP
    run = slots // 2
    vmem = pl.BlockSpec(memory_space=pltpu.VMEM)
    hbm = pl.BlockSpec(memory_space=pltpu.HBM)
    dma = pltpu.SemaphoreType.DMA
    shapes = [
        ((128, count), BF16),
        ((128, count), BF16),
        (route_ids.shape[::-1], jnp.int32),
        (route_ids.shape[::-1], F32),
        ((2, 4, width, hid), BF16),
        ((2, 4, width, hid), BF16),
        ((hid, units), BF16),
        ((hid, units), BF16),
        ((hid, units), BF16),
        ((2, 4, width, hid), BF16),
        ((3, 4, width, hid), BF16),
        ((slots, count), BF16),
        ((2, NODES, CAP, 128), BF16),
        ((2, NODES, CAP, 128), BF16),
        ((2, 2, 2, 4, width, run), BF16),
        ((2, 4, 3, hid // 4, run), F32),
        ((2, 4, 3, hid // 4, run), BF16),
        ((2, 3, 3, hid // 4, run), BF16),
        ((2, 3, hid // 4, run), F32),
        ((2, 3, hid // 4, run), BF16),
        ((2, 3, hid // 4, run), BF16),
        ((2, 2, hid // 4, run), F32),
        ((2, 2, 4, 3, hid // 4, run), BF16),
        ((2, 2, 4, width, run), F32),
        ((2, 2, 4, width, run), BF16),
        ((2, 2, 3, width, run), BF16),
        ((2, NODES, CAP, 128), BF16),
        ((2, NODES, CAP, 128), BF16),
    ]
    sems = [(9,), (2, 7), (2, 7), (2, 2, 3), (2, 2, 3), (2, 2, 4), (2, 2, 4), (2, 2, 3), (2, 2, 3), (2, 2), (2, 2)]
    sems += [(2, 2, 3), (2, 2, 3), (2, 2, 4), (2, 2, 4), (2, 2, 3), (2, 2, 3), (2, 7), (2, 7), (3,), (3,)]
    operands = (
        tokens.T,
        out_grad.T,
        route_ids.T,
        route_weights.T,
        gate_weight.reshape(4, 2, width, hid),
        up_weight.reshape(4, 2, width, hid),
        down_weight.reshape(hid, units),
    )
    results = pl.pallas_call(
        kernel,
        out_shape=(
            jax.ShapeDtypeStruct((width, count), BF16),
            jax.ShapeDtypeStruct((width, count), BF16),
            jax.ShapeDtypeStruct((units, hid), BF16),
            jax.ShapeDtypeStruct((units, hid), BF16),
            jax.ShapeDtypeStruct((hid, units), BF16),
        ),
        in_specs=[hbm] * 7,
        out_specs=(vmem,) * 5,
        scratch_shapes=[pltpu.VMEM(shape, kind) for shape, kind in shapes] + [dma(shape) for shape in sems],
        compiler_params=pltpu.CompilerParams(collective_id=0, has_side_effects=True, vmem_limit_bytes=VMEM_BYTES),
        name="expert_layer",
    )(
        *(pltpu.with_memory_space_constraint(array, pltpu.HBM) for array in operands)
    )
    lo, ig, gg, ug, dg = pl.pallas_call(
        finish,
        out_shape=(
            jax.ShapeDtypeStruct((width, count), BF16),
            jax.ShapeDtypeStruct((width, count), BF16),
            jax.ShapeDtypeStruct((units, hid), BF16),
            jax.ShapeDtypeStruct((units, hid), BF16),
            jax.ShapeDtypeStruct((hid, units), BF16),
        ),
        in_specs=[vmem] * 5,
        out_specs=(hbm,) * 5,
        scratch_shapes=[dma((5,))],
        compiler_params=pltpu.CompilerParams(vmem_limit_bytes=VMEM_BYTES),
        name="finish",
    )(*results)
    return (lo.T, ig.T, gg[None, None], ug[None, None], dg[None, None])


def solution(mesh):
    rows = P("node", "local")
    routes = P("node", None)
    blocks = P("node", "local", None, None)
    return jax.shard_map(
        on_device,
        mesh=mesh,
        in_specs=(rows, rows, routes, routes, blocks, blocks, blocks),
        out_specs=(rows, rows, blocks, blocks, blocks),
        check_vma=False,
    )
```

```python
import jax
import jax.numpy as jnp
from jax import lax
from jax.experimental import pallas as pl
from jax.experimental.pallas import tpu as pltpu
from jax.sharding import PartitionSpec as P

EXPERTS = 256
CAP = 32
VMEM_BYTES = 24 << 20
NODES = 8
MESH = pl.DeviceIdType.MESH
BF16 = jnp.bfloat16
F32 = jnp.float32


def nn(left, right):
    return lax.dot_general(left, right, (((1,), (0,)), ((), ())), preferred_element_type=F32)


def nt(left, right):
    return lax.dot_general(left, right, (((1,), (1,)), ((), ())), preferred_element_type=F32)


def slot_numbers(count):
    return lax.broadcasted_iota(jnp.int32, (NODES * CAP, count), 0).astype(F32)


STEPS = (0, 1, 7, 2, 6, 3, 5, 4)
RUNS = ((0, 4), (4, 8))


def kernel(
    tok_h, og_h, ids_h, wts_h, wg_h, wu_h, wd_h,
    lo, ig, gg, ug, dg,
    tok, og, ids, wts, wg, wu, wd, wgt, wut, wdt, far_w, sel, a_src, a_dst, held,
    c_own, c_src, c_dst, y_own, y_src, y_dst, act, rows, r_own, r_src, r_dst, f_src, f_dst,
    w_sem, as_sem, ar_sem, bs_sem, br_sem, gs_sem, gr_sem, cs_sem, cr_sem, ys_sem, yr_sem,
    ds_sem, dr_sem, es_sem, er_sem, rs_sem, rr_sem, fs_sem, fr_sem, xs_sem, xr_sem,
):
    node = lax.axis_index("node")
    lane = lax.axis_index("local")
    x, half, spot, core = lane // 16, (lane // 8) % 2, (lane // 2) % 4, lane % 2
    unit = lane % 8

    def place(x_at, half_at, spot_at, core_at):
        return {"node": node, "local": ((x_at * 2 + half_at) * 4 + spot_at) * 2 + core_at}

    def after(j):
        return (node + STEPS[j]) % NODES

    def ahead(j):
        return (node + NODES - STEPS[j]) % NODES

    z_peer = [{"node": (node + d) % NODES, "local": lane} for d in range(1, 8)]
    x_peer = [place((x + d) % 4, half, spot, core) for d in range(1, 4)]
    y_peer = [place(x, half, (spot + d) % 4, core) for d in range(1, 4)]
    x_twin = [place((x + d) % 4, half, spot, 1 - core) for d in range(1, 4)]
    twin = place(x, half, spot, 1 - core)
    far = place(x, 1 - half, spot, core)

    barrier = pltpu.get_barrier_semaphore()
    for peer in z_peer + x_peer + x_twin + y_peer + [twin, far]:
        pl.semaphore_signal(barrier, inc=1, device_id=peer, device_id_type=MESH)

    sends = []

    def send(src, dst, s_sem, r_sem, peer):
        copy = pltpu.make_async_remote_copy(
            src_ref=src, dst_ref=dst, send_sem=s_sem, recv_sem=r_sem, device_id=peer, device_id_type=MESH
        )
        copy.start()
        sends.append(copy)
        return copy

    width = tok_h.shape[0]
    units, hid = 8 * width, wd.shape[0]
    slots = NODES * CAP
    run = slots // 2
    count = tok.shape[1]
    loads = [
        pltpu.make_async_copy(src, dst, w_sem.at[i])
        for i, (src, dst) in enumerate(
            [
                (ids_h, ids),
                (wts_h, wts),
                (tok_h, tok.at[pl.ds(0, width)]),
                (og_h, og.at[pl.ds(0, width)]),
                (wg_h.at[:, 0], wg.at[0]),
                (wg_h.at[:, 1], wg.at[1]),
                (wu_h.at[:, 0], wu.at[0]),
                (wu_h.at[:, 1], wu.at[1]),
                (wd_h, wd),
            ]
        )
    ]
    for load in loads:
        load.start()
    tok[pl.ds(width, 128 - width)] = jnp.zeros((128 - width, count), BF16)
    og[pl.ds(width, 128 - width)] = jnp.zeros((128 - width, count), BF16)
    before = lax.broadcasted_iota(jnp.int32, (128, 128), 0) < lax.broadcasted_iota(jnp.int32, (128, 128), 1)
    before = jnp.where(before, 1.0, 0.0).astype(BF16)
    loads[0].wait()

    match = (ids[...] & (EXPERTS // NODES - 1)) == 0
    hit = jnp.sum(jnp.where(match, 1.0, 0.0), axis=0, keepdims=True)
    owner = jnp.sum(jnp.where(match, ids[...] // (EXPERTS // NODES), 0), axis=0, keepdims=True)
    mine = (lax.broadcasted_iota(jnp.int32, (16, count), 0) == owner) & (hit > 0.0)
    mine = jnp.where(mine, 1.0, 0.0)
    blocks = [mine[:, low : low + 128] for low in range(0, count, 128)]
    within = nn(jnp.concatenate(blocks, axis=0).astype(BF16), before)
    rank, passed = [], jnp.zeros((16, 1), F32)
    for b, block in enumerate(blocks):
        rank.append(jnp.sum(block * (within[16 * b : 16 * b + 16] + passed), axis=0, keepdims=True))
        passed = passed + jnp.sum(block, axis=1, keepdims=True)
    rank = jnp.concatenate(rank, axis=1)
    target = jnp.where(hit > 0.0, (owner * CAP).astype(F32) + rank, -1.0)
    sel[...] = jnp.where(slot_numbers(count) == target, 1.0, 0.0).astype(BF16)

    def dispatch(s, source):
        a_src[s] = nt(sel[...], source).astype(BF16).reshape(NODES, CAP, 128)
        copies = [None]
        for j in range(1, 8):
            peer = {"node": ahead(j), "local": lane}
            copies.append(send(a_src.at[s, ahead(j)], a_dst.at[s, j], as_sem.at[s, j - 1], ar_sem.at[s, j - 1], peer))
        a_dst[s, 0] = a_src[s, node]
        return copies

    def gather(s, h, copies):
        low, high = RUNS[h]
        for copy in copies[max(low, 1) : high]:
            copy.wait_recv()
        held[s, h, core, spot] = a_dst[s, low:high].reshape(run, 128).T[0:width]
        own = held.at[s, h, core, spot]
        to_line = [send(own, own, bs_sem.at[s, h, d - 1], br_sem.at[s, h, d - 1], y_peer[d - 1]) for d in range(1, 4)]
        to_twin = send(own, own, gs_sem.at[s, h, 0], gr_sem.at[s, h, 0], twin)
        return to_twin, to_line

    def forward(s, h, state):
        to_twin, to_line = state
        shared = [to_twin]
        for d in range(1, 4):
            to_line[d - 1].wait_recv()
            block = held.at[s, h, core, (spot + 4 - d) % 4]
            shared.append(send(block, block, gs_sem.at[s, h, d], gr_sem.at[s, h, d], twin))
        return shared

    def in_order(blocks):
        return jnp.concatenate([blocks(k, p) for p in range(4) for k in range(2)], axis=0)

    def whole(s, h):
        return in_order(lambda k, p: held[s, h, k, p])

    def all_rows(part):
        return jnp.concatenate([part(h) for h in range(2)], axis=1)

    def scatter(s, h, first, parts):
        for i, part in enumerate(parts):
            split = part.reshape(4, hid // 4, run)
            c_own[h, :, first + i] = split
            c_src[h, :, first + i] = split.astype(BF16)
        span = pl.ds(first, len(parts))
        return [
            send(
                c_src.at[h, (x + d) % 4, span],
                c_dst.at[h, d - 1, span],
                cs_sem.at[s, h, d - 1],
                cr_sem.at[s, h, d - 1],
                x_peer[d - 1],
            )
            for d in range(1, 4)
        ]

    def across(s, h, first, number, copies):
        span = slice(first, first + number)
        total = c_own[h, x, span]
        for d in range(1, 4):
            copies[d - 1].wait_recv()
            total = total + c_dst[h, d - 1, span].astype(F32)
        y_src[h, span] = total.astype(BF16)
        y_own[h, span] = total
        span = pl.ds(first, number)
        return send(y_src.at[h, span], y_dst.at[h, span], ys_sem.at[s, h], yr_sem.at[s, h], far)

    def complete(h, first, number, copy):
        copy.wait_recv()
        return [y_own[h, first + i] + y_dst[h, first + i].astype(F32) for i in range(number)]

    def spread(s, h, first, values):
        for i, value in enumerate(values):
            rows[h, core, x, first + i] = value
        span = pl.ds(first, len(values))
        block = rows.at[h, core, x, span]
        out = [send(block, block, ds_sem.at[s, h, d - 1], dr_sem.at[s, h, d - 1], x_peer[d - 1]) for d in range(1, 4)]
        shared = [send(block, block, es_sem.at[s, h, 0], er_sem.at[s, h, 0], twin)]
        if s == 0:
            shared += [send(block, block, es_sem.at[s, h, d], er_sem.at[s, h, d], x_twin[d - 1]) for d in range(1, 4)]
        return span, out, shared

    def pass_on(s, h, state):
        span, out, shared = state
        for d in range(1, 4):
            out[d - 1].wait_recv()
            if s == 1:
                block = rows.at[h, core, (x + 4 - d) % 4, span]
                shared.append(send(block, block, es_sem.at[s, h, d], er_sem.at[s, h, d], twin))
        return shared

    def gathered(h, which, i):
        return rows[h, which, :, i].reshape(hid, run)

    def line_sum(s, h, terms, shared):
        total = sum(nn(own[core].reshape(4 * width, hid), gathered(h, core, i)) for i, own, _ in terms)
        for copy in shared:
            copy.wait_recv()
        total += sum(nn(far_w[f].reshape(4 * width, hid), gathered(h, 1 - core, i)) for i, _, f in terms)
        total = total.reshape(4, width, run)
        r_src[s, h] = total.astype(BF16)
        r_own[s, h] = total
        return [
            send(
                r_src.at[s, h, (spot + d) % 4],
                r_dst.at[s, h, d - 1],
                rs_sem.at[s, h, d - 1],
                rr_sem.at[s, h, d - 1],
                y_peer[d - 1],
            )
            for d in range(1, 4)
        ]

    def give_back(s, h, copies):
        low, high = RUNS[h]
        total = r_own[s, h, spot]
        for d in range(1, 4):
            copies[d - 1].wait_recv()
            total = total + r_dst[s, h, d - 1].astype(F32)
        f_src[s, low:high, :, 0:width] = total.astype(BF16).T.reshape(high - low, CAP, width)
        out = []
        for j in reversed(range(max(low, 1), high)):
            peer = {"node": after(j), "local": lane}
            out.append(send(f_src.at[s, j], f_dst.at[s, node], fs_sem.at[s, j - 1], fr_sem.at[s, j - 1], peer))
        if low == 0:
            f_dst[s, node] = f_src[s, 0]
        return out

    pl.semaphore_wait(barrier, 18)
    loads[2].wait()
    a_tok = dispatch(0, tok[...])
    loads[1].wait()
    share = jnp.sum(jnp.where(match, wts[...], 0.0), axis=0, keepdims=True)
    loads[3].wait()
    a_grad = dispatch(1, (share * og[...].astype(F32)).astype(BF16))

    for load in loads[4:]:
        load.wait()
    wdt_full = wd[...].T.reshape(4, 2, width, hid)
    wdt[0] = wdt_full[:, 0]
    wdt[1] = wdt_full[:, 1]
    far_copies = [
        send(weight.at[1 - core], far_w.at[i], xs_sem.at[i], xr_sem.at[i], twin) for i, weight in enumerate((wdt, wg, wu))
    ]
    wgt[...] = in_order(lambda k, p: wg[k, p]).T
    wut[...] = in_order(lambda k, p: wu[k, p]).T
    b_tok = [gather(0, h, a_tok) for h in range(2)]
    b_tok = [forward(0, h, b_tok[h]) for h in range(2)]
    b_grad = [gather(1, h, a_grad) for h in range(2)]
    c_fwd, c_bwd, y_fwd, y_bwd, d_fwd, d_bwd = [], [], [], [], [], []
    for h in range(2):
        for copy in b_tok[h]:
            copy.wait_recv()
        tokens = whole(0, h)
        c_fwd.append(scatter(0, h, 0, [nn(wgt[...], tokens), nn(wut[...], tokens)]))

    def activate(h):
        gate_sum, up_sum = complete(h, 0, 2, y_fwd[h])
        sig = jax.nn.sigmoid(gate_sum)
        active = gate_sum * sig
        d_fwd.append(spread(0, h, 0, [(active * up_sum).astype(BF16)]))
        act[h, 0] = up_sum * sig * (1.0 + gate_sum * (1.0 - sig))
        act[h, 1] = active

    def differentiate(h):
        (back_sum,) = complete(h, 2, 1, y_bwd[h])
        d_bwd.append(spread(1, h, 1, [(back_sum * act[h, 0]).astype(BF16), (back_sum * act[h, 1]).astype(BF16)]))

    for h in range(2):
        b_grad[h] = forward(1, h, b_grad[h])
        y_fwd.append(across(0, h, 0, 2, c_fwd[h]))
        for copy in b_grad[h]:
            copy.wait_recv()
        c_bwd.append(scatter(1, h, 2, [nn(wd[...], whole(1, h))]))
    for h in range(2):
        y_bwd.append(across(1, h, 2, 1, c_bwd[h]))
        activate(h)
    for copy in far_copies:
        copy.wait_recv()
    r_fwd, r_bwd, f_fwd, f_bwd = [], [], [], []
    for h in range(2):
        shared = pass_on(0, h, d_fwd[h])
        differentiate(h)
        r_fwd.append(line_sum(0, h, [(0, wdt, 0)], shared))
    for h in range(2):
        shared = pass_on(1, h, d_bwd[h])
        r_bwd.append(line_sum(1, h, [(1, wg, 1), (2, wu, 2)], shared))
    dg[...] = nt(all_rows(lambda h: gathered(h, core, 0)), all_rows(lambda h: whole(1, h))).astype(BF16)
    tokens = all_rows(lambda h: whole(0, h))
    for h in range(2):
        f_fwd += give_back(0, h, r_fwd[h])
    gg[...] = nt(tokens, all_rows(lambda h: gathered(h, core, 1))).astype(BF16)
    ug[...] = nt(tokens, all_rows(lambda h: gathered(h, core, 2))).astype(BF16)
    for h in range(2):
        f_bwd += give_back(1, h, r_bwd[h])

    def combine(s, copies):
        for copy in copies:
            copy.wait_recv()
        return nn(f_dst[s, :, :, 0:width].reshape(slots, width).T, sel[...])

    lo[...] = (share * combine(0, f_fwd)).astype(BF16)
    ig[...] = combine(1, f_bwd).astype(BF16)
    for copy in sends:
        copy.wait_send()


def finish(*refs):
    count = len(refs) // 2
    copies = [pltpu.make_async_copy(refs[i], refs[count + i], refs[-1].at[i]) for i in range(count)]
    for copy in copies:
        copy.start()
    for copy in copies:
        copy.wait()


def on_device(tokens, out_grad, route_ids, route_weights, gate_weight, up_weight, down_weight):
    count, width = tokens.shape
    units, hid = gate_weight.shape[2], gate_weight.shape[3]
    slots = NODES * CAP
    run = slots // 2
    vmem = pl.BlockSpec(memory_space=pltpu.VMEM)
    hbm = pl.BlockSpec(memory_space=pltpu.HBM)
    dma = pltpu.SemaphoreType.DMA
    shapes = [
        ((128, count), BF16),
        ((128, count), BF16),
        (route_ids.shape[::-1], jnp.int32),
        (route_ids.shape[::-1], F32),
        ((2, 4, width, hid), BF16),
        ((2, 4, width, hid), BF16),
        ((hid, units), BF16),
        ((hid, units), BF16),
        ((hid, units), BF16),
        ((2, 4, width, hid), BF16),
        ((3, 4, width, hid), BF16),
        ((slots, count), BF16),
        ((2, NODES, CAP, 128), BF16),
        ((2, NODES, CAP, 128), BF16),
        ((2, 2, 2, 4, width, run), BF16),
        ((2, 4, 3, hid // 4, run), F32),
        ((2, 4, 3, hid // 4, run), BF16),
        ((2, 3, 3, hid // 4, run), BF16),
        ((2, 3, hid // 4, run), F32),
        ((2, 3, hid // 4, run), BF16),
        ((2, 3, hid // 4, run), BF16),
        ((2, 2, hid // 4, run), F32),
        ((2, 2, 4, 3, hid // 4, run), BF16),
        ((2, 2, 4, width, run), F32),
        ((2, 2, 4, width, run), BF16),
        ((2, 2, 3, width, run), BF16),
        ((2, NODES, CAP, 128), BF16),
        ((2, NODES, CAP, 128), BF16),
    ]
    sems = [(9,), (2, 7), (2, 7), (2, 2, 3), (2, 2, 3), (2, 2, 4), (2, 2, 4), (2, 2, 3), (2, 2, 3), (2, 2), (2, 2)]
    sems += [(2, 2, 3), (2, 2, 3), (2, 2, 4), (2, 2, 4), (2, 2, 3), (2, 2, 3), (2, 7), (2, 7), (3,), (3,)]
    operands = (
        tokens.T,
        out_grad.T,
        route_ids.T,
        route_weights.T,
        gate_weight.reshape(4, 2, width, hid),
        up_weight.reshape(4, 2, width, hid),
        down_weight.reshape(hid, units),
    )
    results = pl.pallas_call(
        kernel,
        out_shape=(
            jax.ShapeDtypeStruct((width, count), BF16),
            jax.ShapeDtypeStruct((width, count), BF16),
            jax.ShapeDtypeStruct((units, hid), BF16),
            jax.ShapeDtypeStruct((units, hid), BF16),
            jax.ShapeDtypeStruct((hid, units), BF16),
        ),
        in_specs=[hbm] * 7,
        out_specs=(vmem,) * 5,
        scratch_shapes=[pltpu.VMEM(shape, kind) for shape, kind in shapes] + [dma(shape) for shape in sems],
        compiler_params=pltpu.CompilerParams(collective_id=0, has_side_effects=True, vmem_limit_bytes=VMEM_BYTES),
        name="expert_layer",
    )(
        *(pltpu.with_memory_space_constraint(array, pltpu.HBM) for array in operands)
    )
    lo, ig, gg, ug, dg = pl.pallas_call(
        finish,
        out_shape=(
            jax.ShapeDtypeStruct((width, count), BF16),
            jax.ShapeDtypeStruct((width, count), BF16),
            jax.ShapeDtypeStruct((units, hid), BF16),
            jax.ShapeDtypeStruct((units, hid), BF16),
            jax.ShapeDtypeStruct((hid, units), BF16),
        ),
        in_specs=[vmem] * 5,
        out_specs=(hbm,) * 5,
        scratch_shapes=[dma((5,))],
        compiler_params=pltpu.CompilerParams(vmem_limit_bytes=VMEM_BYTES),
        name="finish",
    )(*results)
    return (lo.T, ig.T, gg[None, None], ug[None, None], dg[None, None])


def solution(mesh):
    rows = P("node", "local")
    routes = P("node", None)
    blocks = P("node", "local", None, None)
    return jax.shard_map(
        on_device,
        mesh=mesh,
        in_specs=(rows, rows, routes, routes, blocks, blocks, blocks),
        out_specs=(rows, rows, blocks, blocks, blocks),
        check_vma=False,
    )
```
